32 devices in a mesh: dp: 8 (over z, y), cuts: 4 (over x, core).
Axes of the slice: x: 2, y: 2, z: 4, core: 2. Of those that a mesh axis runs over, the one named last changes fastest.
Arguments:
- tokens: bfloat16 [128, 6144], P('dp', 'cuts'), may hold values from -6 to 6
- out_grad: bfloat16 [128, 6144], P('dp', 'cuts'), may hold values from -6 to 6
- gate_values: float32 [128, 2], P('dp'), may hold values from 0.2 to 1
- routing: int32 [128, 2], P('dp'), may hold values from 0 to 7, all different within a row; in each aligned block of 16 rows (0 to 15, 16 to 31, ...) at most 8 rows name the same one
- gate_weight: bfloat16 [8, 6144, 11264], P('dp', None, 'cuts'), may hold values from -0.078125 to 0.078125
- up_weight: bfloat16 [8, 6144, 11264], P('dp', None, 'cuts'), may hold values from -0.078125 to 0.078125
- down_weight: bfloat16 [8, 11264, 6144], P('dp', 'cuts'), may hold values from -0.0546875 to 0.0546875
Outputs:
- mixed: bfloat16 [128, 6144], P('dp', 'cuts')
- token_grad: bfloat16 [128, 6144], P('dp', 'cuts')
The draws below stay inside these ranges and needn't reach their ends.
Inputs may be any that keep to these rules, and one draw needn't show every extreme that they name: `routing`: each row names 2 different experts; in each aligned block of 16 rows (the rows of one index of dp) no expert is named by more than 8 rows, and in some block one expert is named by exactly 8 rows.
All inputs are finite; a program needn't handle non-finite values.
Results may differ from the reference program's by a relative error of at most 0.019.
Values may be sent and summed in bfloat16 or wider, within the bound.
A program may use at most 192 MiB of HBM per device.

```python
import math
import jax
import jax.numpy as jnp
import numpy as np
from jax import lax

D = 6144
E = 8
TOPK = 2
FF = 11264
TOK = 16
CAP = 8
TOKENS = 128
SUBS = 1
FFQ = 11264
HID = 2816
SLOTS = 64
N_DP = 8


def steps_of(key, dims, cuts, smallest, largest):
    gain, own = 1.0, jax.random.fold_in(key, 6)
    for axis_at, blocks in cuts:
        heights = jnp.exp(jax.random.uniform(jax.random.fold_in(own, axis_at), (blocks,), jnp.float32, smallest / len(cuts), largest / len(cuts)))
        gain = gain * jnp.repeat(heights, dims[axis_at] // blocks).reshape([-1 if axis == axis_at else 1 for axis in range(len(dims))])
    return gain


def shared_out(key, own, number, rows, count, top, reach, lean):
    sequence = jax.random.permutation(key, count)
    packed, common = portions_of(count, rows * top, reach, lean, True), portions_of(count, rows * top, reach, lean, False)
    places = jnp.arange(count)

    def named(sizes, offset_by):
        used = int((sizes > 0).sum())
        fixed = max(1, used // 4)
        shifted = fixed + (places - fixed + offset_by * (used - fixed)) % max(1, count - fixed)
        return jnp.zeros((count,), jnp.int32).at[sequence[jnp.where(places < fixed, places, shifted)]].set(jnp.asarray(sizes, jnp.int32))

    sizes = jnp.where(number % 4 == 0, named(packed, number // 4), named(common, number - number // 4 - 1))
    mixed = jax.random.permutation(jax.random.fold_in(own, 3), count)
    donor, receiver = mixed[0:count // 2 * 2:2], mixed[1:count // 2 * 2:2]
    margin = jnp.minimum(sizes[donor] - 1, reach - sizes[receiver]) // 2
    margin = jnp.where((donor == sequence[0]) | (receiver == sequence[0]) | (sizes[receiver] == 0), 0, jnp.maximum(margin, 0))
    shifted = jax.random.randint(jax.random.fold_in(own, 4), (count // 2,), 0, 1 << 20) % (margin + 1)
    sizes = sizes.at[donor].add(-shifted).at[receiver].add(shifted)
    labels = jnp.searchsorted(jnp.cumsum(sizes), jnp.arange(rows * top), side="right").astype(jnp.int32)
    table = labels.reshape(top, rows).T
    table = table[jax.random.permutation(jax.random.fold_in(own, 1), rows)]
    offset_by = jax.random.randint(jax.random.fold_in(own, 2), (rows, 1), 0, top)
    return jnp.take_along_axis(table, (jnp.arange(top)[None, :] + offset_by) % top, axis=1)


def portions_of(amount, total, limit, skew, full):
    portions = [(1 << 20) // math.isqrt(standing ** skew) + 1 for standing in range(1, amount + 1)]
    largest = limit if full else min(limit, max(-(-total // amount), total * portions[0] // sum(portions)))
    least = 1 if total - largest >= amount - 1 else 0
    given, surplus = [largest] + [least] * (amount - 1), total - largest - least * (amount - 1)
    while surplus > 0:
        candidates = [i for i in range(1, amount) if given[i] < largest] or [i for i in range(1, amount) if given[i] < limit]
        mass, budget = sum([portions[i] for i in candidates]), surplus
        for i in candidates:
            more = min(limit - given[i], max(1, budget * portions[i] // mass), surplus)
            given[i] = given[i] + more
            surplus = surplus - more
    return np.array(given)


def gaussian(rng, dims, scale, limit, pieces=(), kind=jnp.bfloat16):
    drawn = jax.random.normal(rng, dims, jnp.float32) * scale
    if len(pieces) > 0:
        drawn = steps_of(rng, dims, pieces, -0.22, 0.18) * drawn
    return jnp.clip(drawn, min=-limit, max=limit).astype(kind)


def setup_inputs(seed: int = 0) -> dict:
    arg_keys = jax.random.split(jax.random.key(seed), 8)
    tokens = gaussian(arg_keys[0], (TOKENS, D), 1.0, 6.0, ((0, 8), (1, 4)))
    out_grad = gaussian(arg_keys[1], (TOKENS, D), 1.0, 6.0, ((0, 8), (1, 4)))
    gate_values = jnp.clip(0.2 + 0.8 * jax.random.uniform(arg_keys[2], (TOKENS, TOPK), jnp.float32) ** steps_of(arg_keys[2], (TOKENS, TOPK), ((0, 8),), -0.2, 0.2), 0.2, 1.0)
    routing_keys = jax.random.split(jax.random.fold_in(arg_keys[3], 1), TOKENS // TOK)
    routing_turns = jax.random.permutation(jax.random.fold_in(arg_keys[3], 3), TOKENS // TOK)
    routing = jax.vmap(lambda own, number: shared_out(jax.random.fold_in(arg_keys[3], 2), own, number, TOK, E, TOPK, CAP, 2))(routing_keys, routing_turns).reshape((TOKENS, TOPK))
    gate_weight = gaussian(arg_keys[4], (N_DP, D, FFQ), D ** -0.5, 0.078125, ((0, 8), (2, 4)))
    up_weight = gaussian(arg_keys[5], (N_DP, D, FFQ), D ** -0.5, 0.078125, ((0, 8), (2, 4)))
    down_weight = gaussian(arg_keys[6], (N_DP, FFQ, D), FF ** -0.5, 0.0546875, ((0, 8), (1, 4)))
    return {"tokens": tokens, "out_grad": out_grad, "gate_values": gate_values, "routing": routing, "gate_weight": gate_weight, "up_weight": up_weight, "down_weight": down_weight}


def expert_weights(gate_weight, up_weight, down_weight, expert):
    wg = jnp.concatenate([gate_weight[expert * SUBS + s] for s in range(SUBS)], axis=1)
    wu = jnp.concatenate([up_weight[expert * SUBS + s] for s in range(SUBS)], axis=1)
    w2 = jnp.concatenate([down_weight[expert * SUBS + s] for s in range(SUBS)], axis=0)
    return wg, wu, w2


def reference(tokens, out_grad, gate_values, routing, gate_weight, up_weight, down_weight):
    pair_count = TOKENS * TOPK
    experts = routing.reshape(-1)
    pairs_x = jnp.concatenate([jnp.repeat(tokens, TOPK, axis=0), jnp.zeros((1, D), jnp.bfloat16)], axis=0)
    scaled = (gate_values[:, :, None] * out_grad[:, None, :].astype(jnp.float32)).astype(jnp.bfloat16)
    scaled = jnp.concatenate([scaled.reshape(pair_count, D), jnp.zeros((1, D), jnp.bfloat16)], axis=0)
    y_pairs = jnp.zeros((pair_count + 1, D), jnp.float32)
    dx_pairs = jnp.zeros((pair_count + 1, D), jnp.float32)
    blocks = FF // HID
    contract = (((1,), (1,)), ((), ()))
    for expert in range(E):
        index = jnp.nonzero(experts == expert, size=SLOTS, fill_value=pair_count)[0].astype(jnp.int32)
        rows_x = pairs_x[index]
        rows_dy = scaled[index]
        wg, wu, w2 = expert_weights(gate_weight, up_weight, down_weight, expert)
        gate_pre = jnp.dot(rows_x, wg, preferred_element_type=jnp.float32)
        up_pre = jnp.dot(rows_x, wu, preferred_element_type=jnp.float32)
        sigma = jax.nn.sigmoid(gate_pre)
        silu = gate_pre * sigma
        hidden = (silu * up_pre).astype(jnp.bfloat16)
        hid_grad = lax.dot_general(rows_dy, w2, contract, preferred_element_type=jnp.float32)
        gate_grad = (hid_grad * up_pre * sigma * (1.0 + gate_pre * (1.0 - sigma))).astype(jnp.bfloat16)
        up_grad = (hid_grad * silu).astype(jnp.bfloat16)

        def block_term(carry, block):
            start = block * HID
            hid_block = lax.dynamic_slice_in_dim(hidden, start, HID, 1)
            down_block = lax.dynamic_slice_in_dim(w2, start, HID, 0)
            out_part = jnp.dot(hid_block, down_block, preferred_element_type=jnp.float32).astype(jnp.bfloat16)
            gg_block = lax.dynamic_slice_in_dim(gate_grad, start, HID, 1)
            ug_block = lax.dynamic_slice_in_dim(up_grad, start, HID, 1)
            wg_block = lax.dynamic_slice_in_dim(wg, start, HID, 1)
            wu_block = lax.dynamic_slice_in_dim(wu, start, HID, 1)
            in_part = lax.dot_general(gg_block, wg_block, contract, preferred_element_type=jnp.float32)
            in_part = in_part + lax.dot_general(ug_block, wu_block, contract, preferred_element_type=jnp.float32)
            in_part = in_part.astype(jnp.bfloat16)
            out_part, in_part = lax.optimization_barrier((out_part, in_part))
            return (carry[0] + out_part.astype(jnp.float32), carry[1] + in_part.astype(jnp.float32)), None

        start_sums = (jnp.zeros((SLOTS, D), jnp.float32), jnp.zeros((SLOTS, D), jnp.float32))
        sums, unused = lax.scan(block_term, start_sums, jnp.arange(blocks, dtype=jnp.int32))
        y_pairs = y_pairs.at[index].add(sums[0])
        dx_pairs = dx_pairs.at[index].add(sums[1])
    mixed = jnp.sum(y_pairs[:pair_count].reshape(TOKENS, TOPK, D) * gate_values[:, :, None], axis=1)
    token_grad = jnp.sum(dx_pairs[:pair_count].reshape(TOKENS, TOPK, D), axis=1)
    return mixed.astype(jnp.bfloat16), token_grad.astype(jnp.bfloat16)
```

```python
import functools

import jax
import jax.numpy as jnp
from jax import lax
from jax.experimental import pallas as pl
from jax.experimental.pallas import tpu as pltpu
from jax.sharding import PartitionSpec as P

E = 8
TOPK = 2
CAP = 8
MESH = pl.DeviceIdType.MESH
F32 = jnp.float32
BF16 = jnp.bfloat16
NT = (((1,), (1,)), ((), ()))


def slot_table(routing):
    experts = routing.reshape(-1)
    pairs = experts.shape[0]
    at = jnp.arange(pairs, dtype=jnp.int32)
    same = (experts[:, None] == experts[None, :]) & (at[None, :] < at[:, None])
    slots = (experts * CAP + jnp.sum(same.astype(jnp.int32), axis=1)).reshape(routing.shape)
    numbers = jnp.arange(E * CAP, dtype=jnp.int32)
    takes = [(numbers[:, None] == slots[:, k][None, :]).astype(BF16) for k in range(TOPK)]
    gives = [(slots[:, k][:, None] == numbers[None, :]).astype(BF16) for k in range(TOPK)]
    return takes + gives


def body(
    n, cuts, tile, depth,
    x_ref, dy_ref, gate_ref, take0, take1, give0, give1, wg_hbm, wu_hbm, w2_hbm,
    mixed_ref, grad_ref,
    wg, wu, w2, send, rx, rows_x, rows_dy, acc_y, acc_dx,
    core_tx, core_rx, x_tx, x_rx, own, back_tx, back_rx,
    w_sem, a_send, a_recv, b_send, b_recv, c_send, c_recv, f_send, f_recv,
    r1_send, r1_recv, r2_send, r2_recv, r3_send, r3_recv,
):
    me, cut = lax.axis_index("dp"), lax.axis_index("cuts")
    nx = cuts // 2
    core, xx = lax.rem(cut, 2), lax.div(cut, 2)
    owners = n // E
    width = x_ref.shape[1]
    tiles = wg_hbm.shape[2] // tile
    mate = (me, xx * 2 + 1 - core)

    def fetch(t, slot):
        cols = pl.ds(t * tile, tile) if tiles == 1 else pl.ds(pl.multiple_of(t * tile, tile), tile)
        return (
            pltpu.make_async_copy(wg_hbm.at[0, :, cols], wg.at[slot], w_sem.at[0, slot]),
            pltpu.make_async_copy(wu_hbm.at[0, :, cols], wu.at[slot], w_sem.at[1, slot]),
            pltpu.make_async_copy(w2_hbm.at[0, cols, :], w2.at[slot], w_sem.at[2, slot]),
        )

    for t in range(min(depth, tiles)):
        for copy in fetch(t, t):
            copy.start()

    barrier = pltpu.get_barrier_semaphore()

    def greet(j, carry):
        pl.semaphore_signal(barrier, inc=1, device_id=(lax.rem(me + j, n), cut), device_id_type=MESH)
        return carry

    lax.fori_loop(1, n, greet, 0)
    pl.semaphore_signal(barrier, inc=1, device_id=mate, device_id_type=MESH)
    for i in range(1, nx):
        pl.semaphore_signal(
            barrier, inc=1, device_id=(me, lax.rem(xx + i, nx) * 2 + core), device_id_type=MESH
        )

    x = x_ref[...]
    dy = dy_ref[...].astype(F32)
    gate = gate_ref[...]
    sent_x = jnp.dot(take0[...] + take1[...], x, preferred_element_type=F32)
    sent_dy = jnp.dot(take0[...], (gate[:, 0:1] * dy).astype(BF16), preferred_element_type=F32)
    sent_dy += jnp.dot(take1[...], (gate[:, 1:2] * dy).astype(BF16), preferred_element_type=F32)
    send[...] = jnp.concatenate(
        [sent_x.reshape(E, CAP, width), sent_dy.reshape(E, CAP, width)], axis=1
    ).astype(BF16)
    rx[cut, me] = send[lax.div(me, owners)]

    pl.semaphore_wait(barrier, (n - 1) + 1 + (nx - 1))

    def remote(src, dst, send_sem, recv_sem, device):
        return pltpu.make_async_remote_copy(
            src_ref=src, dst_ref=dst, send_sem=send_sem, recv_sem=recv_sem,
            device_id=device, device_id_type=MESH,
        )

    def source(j):
        return lax.rem(me - j + n, n)

    def copy_a(j):
        to = lax.rem(me + j, n)
        return remote(send.at[lax.div(to, owners)], rx.at[cut, me], a_send.at[j], a_recv.at[j], (to, cut))

    def copy_b(j):
        s = source(j)
        return remote(rx.at[cut, s], rx.at[cut, s], b_send.at[j], b_recv.at[j], mate)

    def copy_c(i, j):
        s = source(j)
        to = (me, lax.rem(xx + i, nx) * 2 + core)
        return remote(rx.at[cut, s], rx.at[cut, s], c_send.at[i - 1, j], c_recv.at[i - 1, j], to)

    def copy_f(i, j):
        s = source(j)
        part = lax.rem(xx - i + nx, nx) * 2 + core
        return remote(rx.at[part, s], rx.at[part, s], f_send.at[i - 1, j], f_recv.at[i - 1, j], mate)

    def loop(start, stop, step):
        def run(j, carry):
            step(j)
            return carry

        lax.fori_loop(start, stop, run, 0)

    def spread(j):
        for i in range(1, nx):
            copy_c(i, j).start()
        copy_b(j).start()

    def arrive(j):
        copy_a(j).wait_recv()
        spread(j)

    def forward(j):
        for i in range(1, nx):
            copy_c(i, j).wait_recv()
            copy_f(i, j).start()

    def both(j):
        arrive(j)
        forward(j - 2)

    def landed(j):
        copy_b(j).wait_recv()
        for i in range(1, nx):
            copy_f(i, j).wait_recv()

    loop(1, n, lambda j: copy_a(j).start())
    spread(0)
    arrive(1)
    acc_y[...] = jnp.zeros_like(acc_y)
    acc_dx[...] = jnp.zeros_like(acc_dx)
    loop(2, n, both)
    loop(n - 2, n, forward)
    loop(0, n, landed)

    for part in range(cuts):
        cols = slice(part * width, (part + 1) * width)
        got = rx[part].astype(F32)
        rows_x[:, cols] = got[:, :CAP].reshape(n * CAP, width).astype(BF16)
        rows_dy[:, cols] = got[:, CAP:].reshape(n * CAP, width).astype(BF16)

    def hidden_tile(t):
        slot = lax.rem(t, depth)
        for copy in fetch(t, slot):
            copy.wait()
        gate_pre = jnp.dot(rows_x[...], wg[slot], preferred_element_type=F32)
        up_pre = jnp.dot(rows_x[...], wu[slot], preferred_element_type=F32)
        hid_grad = lax.dot_general(rows_dy[...], w2[slot], NT, preferred_element_type=F32)
        sigma = 1.0 / (1.0 + jnp.exp(-gate_pre))
        silu = gate_pre * sigma
        hidden = (silu * up_pre).astype(BF16)
        gate_grad = (hid_grad * up_pre * sigma * (1.0 + gate_pre * (1.0 - sigma))).astype(BF16)
        up_grad = (hid_grad * silu).astype(BF16)
        for part in range(cuts):
            cols = slice(part * width, (part + 1) * width)
            acc_y[:, cols] += jnp.dot(hidden, w2[slot, :, cols], preferred_element_type=F32)
            acc_dx[:, cols] += lax.dot_general(
                gate_grad, wg[slot, cols, :], NT, preferred_element_type=F32
            ) + lax.dot_general(up_grad, wu[slot, cols, :], NT, preferred_element_type=F32)

        @pl.when(t + depth < tiles)
        def _():
            for copy in fetch(t + depth, slot):
                copy.start()

    loop(0, tiles, hidden_tile)

    def partial(part):
        cols = pl.ds(pl.multiple_of(part * width, 128), width)
        return jnp.concatenate(
            [acc_y[:, cols].reshape(n, CAP, width), acc_dx[:, cols].reshape(n, CAP, width)], axis=1
        )

    def copy_r1(p):
        return remote(core_tx.at[p], core_rx.at[p], r1_send.at[p], r1_recv.at[p], mate)

    def copy_r2(i, d):
        to = (me, lax.rem(xx + i, nx) * 2 + core)
        return remote(
            x_tx.at[i - 1, d], x_rx.at[i - 1, d], r2_send.at[i - 1, d], r2_recv.at[i - 1, d], to
        )

    def copy_r3(j):
        to = lax.rem(me + j, n)
        return remote(back_tx.at[to], back_rx.at[me], r3_send.at[j], r3_recv.at[j], (to, cut))

    for i in list(range(1, nx)) + [0]:
        p = lax.rem(xx + i, nx)
        core_tx[p] = partial(p * 2 + 1 - core).astype(BF16)
        copy_r1(p).start()
    for i in list(range(1, nx)) + [0]:
        p = lax.rem(xx + i, nx)
        mine = partial(p * 2 + core)
        copy_r1(p).wait_recv()
        mine = mine + core_rx[p].astype(F32)
        if i == 0:
            own[...] = mine
        else:
            x_tx[i - 1] = mine.astype(BF16)
            loop(1, n + 1, lambda j, i=i: copy_r2(i, lax.rem(me + j, n)).start())

    def total(d):
        value = own[d]
        for i in range(1, nx):
            copy_r2(i, d).wait_recv()
            value = value + x_rx[i - 1, d].astype(F32)
        return value.astype(BF16)

    def give_back(j):
        d = lax.rem(me + j, n)
        back_tx[d] = total(d)
        copy_r3(j).start()

    loop(1, n, give_back)
    back_rx[me] = total(me)
    loop(1, n, lambda j: copy_r3(j).wait_recv())

    back = back_rx[...].astype(F32).reshape(E, owners, 2 * CAP, width)
    mixed = jnp.zeros(mixed_ref.shape, F32)
    grad = jnp.zeros(grad_ref.shape, F32)
    for o in range(owners):
        y = back[:, o, :CAP].reshape(E * CAP, width).astype(BF16)
        dx = back[:, o, CAP:].reshape(E * CAP, width).astype(BF16)
        mixed += gate[:, 0:1] * jnp.dot(give0[...], y, preferred_element_type=F32)
        mixed += gate[:, 1:2] * jnp.dot(give1[...], y, preferred_element_type=F32)
        grad += jnp.dot(give0[...] + give1[...], dx, preferred_element_type=F32)
    mixed_ref[...] = mixed.astype(BF16)
    grad_ref[...] = grad.astype(BF16)

    loop(1, n, lambda j: copy_a(j).wait_send())
    loop(0, n, lambda j: copy_b(j).wait_send())
    for i in range(1, nx):
        loop(0, n, lambda j, i=i: copy_c(i, j).wait_send())
        loop(0, n, lambda j, i=i: copy_f(i, j).wait_send())
        loop(0, n, lambda j, i=i: copy_r2(i, j).wait_send())
    for p in range(nx):
        copy_r1(p).wait_send()
    loop(1, n, lambda j: copy_r3(j).wait_send())


def on_device(n, cuts, tokens, out_grad, gate_values, routing, gate_weight, up_weight, down_weight):
    tables = slot_table(routing)
    count, width = tokens.shape
    _, model, hid = gate_weight.shape
    tile = 256 if hid % 256 == 0 else hid
    depth = min(4, hid // tile)
    nx, rows = cuts // 2, n * CAP
    chunk = (2 * CAP, width)
    dma = pltpu.SemaphoreType.DMA
    vmem = pl.BlockSpec(memory_space=pltpu.VMEM)
    hbm = pl.BlockSpec(memory_space=pl.ANY)
    out = jax.ShapeDtypeStruct((count, width), BF16)
    return pl.pallas_call(
        functools.partial(body, n, cuts, tile, depth),
        out_shape=(out, out),
        in_specs=[vmem] * 7 + [hbm] * 3,
        out_specs=(vmem, vmem),
        scratch_shapes=[
            pltpu.VMEM((depth, model, tile), BF16),
            pltpu.VMEM((depth, model, tile), BF16),
            pltpu.VMEM((depth, tile, model), BF16),
            pltpu.VMEM((E,) + chunk, BF16),
            pltpu.VMEM((cuts, n) + chunk, BF16),
            pltpu.VMEM((rows, model), BF16),
            pltpu.VMEM((rows, model), BF16),
            pltpu.VMEM((rows, model), F32),
            pltpu.VMEM((rows, model), F32),
            pltpu.VMEM((nx, n) + chunk, BF16),
            pltpu.VMEM((nx, n) + chunk, BF16),
            pltpu.VMEM((nx - 1, n) + chunk, BF16),
            pltpu.VMEM((nx - 1, n) + chunk, BF16),
            pltpu.VMEM((n,) + chunk, F32),
            pltpu.VMEM((n,) + chunk, BF16),
            pltpu.VMEM((n,) + chunk, BF16),
            dma((3, depth)),
            dma((n,)), dma((n,)),
            dma((n,)), dma((n,)),
            dma((nx - 1, n)), dma((nx - 1, n)),
            dma((nx - 1, n)), dma((nx - 1, n)),
            dma((nx,)), dma((nx,)),
            dma((nx - 1, n)), dma((nx - 1, n)),
            dma((n,)), dma((n,)),
        ],
        compiler_params=pltpu.CompilerParams(
            collective_id=0, has_side_effects=True, vmem_limit_bytes=62 * 1024 * 1024
        ),
        cost_estimate=pl.CostEstimate(
            flops=12 * rows * model * hid, bytes_accessed=6 * model * hid, transcendentals=rows * hid
        ),
    )(tokens, out_grad, gate_values, *tables, gate_weight, up_weight, down_weight)


def solution(mesh):
    return jax.shard_map(
        functools.partial(on_device, mesh.shape["dp"], mesh.shape["cuts"]),
        mesh=mesh,
        in_specs=(
            P("dp", "cuts"),
            P("dp", "cuts"),
            P("dp", None),
            P("dp", None),
            P("dp", None, "cuts"),
            P("dp", None, "cuts"),
            P("dp", "cuts", None),
        ),
        out_specs=(P("dp", "cuts"), P("dp", "cuts")),
        check_vma=False,
    )
```

```python
import functools

import jax
import jax.numpy as jnp
from jax import lax
from jax.experimental import pallas as pl
from jax.experimental.pallas import tpu as pltpu
from jax.sharding import PartitionSpec as P

E = 8
TOPK = 2
CAP = 8
MESH = pl.DeviceIdType.MESH
F32 = jnp.float32
BF16 = jnp.bfloat16


def slot_table(routing):
    experts = routing.reshape(-1)
    pairs = experts.shape[0]
    at = jnp.arange(pairs, dtype=jnp.int32)
    same = (experts[:, None] == experts[None, :]) & (at[None, :] < at[:, None])
    slots = (experts * CAP + jnp.sum(same.astype(jnp.int32), axis=1)).reshape(routing.shape)
    numbers = jnp.arange(E * CAP, dtype=jnp.int32)
    takes = [(numbers[:, None] == slots[:, k][None, :]).astype(BF16) for k in range(TOPK)]
    gives = [(slots[:, k][:, None] == numbers[None, :]).astype(BF16) for k in range(TOPK)]
    return takes + gives


def body(
    n, cuts, tile, depth,
    x_ref, dy_ref, gate_ref, take0, take1, give0, give1, wg_hbm, wu_hbm, w2_hbm,
    mixed_ref, grad_ref,
    wg, wu, w2, send, rx, rows_x, turned_dy, acc_y, acc_dx,
    core_tx, core_rx, x_tx, x_rx, own, back_tx, back_rx,
    w_sem, a_send, a_recv, b_send, b_recv, c_send, c_recv, f_send, f_recv,
    r1_send, r1_recv, r2_send, r2_recv, r3_send, r3_recv,
):
    me, cut = lax.axis_index("dp"), lax.axis_index("cuts")
    nx = cuts // 2
    core, xx = lax.rem(cut, 2), lax.div(cut, 2)
    owners = n // E
    width = x_ref.shape[1]
    tiles = wg_hbm.shape[2] // tile
    mate = (me, xx * 2 + 1 - core)

    def fetch(t, slot):
        cols = pl.ds(t * tile, tile) if tiles == 1 else pl.ds(pl.multiple_of(t * tile, tile), tile)
        return (
            pltpu.make_async_copy(wg_hbm.at[0, :, cols], wg.at[slot], w_sem.at[0, slot]),
            pltpu.make_async_copy(wu_hbm.at[0, :, cols], wu.at[slot], w_sem.at[1, slot]),
            pltpu.make_async_copy(w2_hbm.at[0, cols, :], w2.at[slot], w_sem.at[2, slot]),
        )

    for t in range(min(depth, tiles)):
        for copy in fetch(t, t):
            copy.start()

    barrier = pltpu.get_barrier_semaphore()

    def greet(j, carry):
        pl.semaphore_signal(barrier, inc=1, device_id=(lax.rem(me + j, n), cut), device_id_type=MESH)
        return carry

    lax.fori_loop(1, n, greet, 0)
    pl.semaphore_signal(barrier, inc=1, device_id=mate, device_id_type=MESH)
    for i in range(1, nx):
        pl.semaphore_signal(
            barrier, inc=1, device_id=(me, lax.rem(xx + i, nx) * 2 + core), device_id_type=MESH
        )

    x = x_ref[...]
    dy = dy_ref[...].astype(F32)
    gate = gate_ref[...]
    sent_x = jnp.dot(take0[...] + take1[...], x, preferred_element_type=F32)
    sent_dy = jnp.dot(take0[...], (gate[:, 0:1] * dy).astype(BF16), preferred_element_type=F32)
    sent_dy += jnp.dot(take1[...], (gate[:, 1:2] * dy).astype(BF16), preferred_element_type=F32)
    send[...] = jnp.concatenate(
        [sent_x.reshape(E, CAP, width), sent_dy.reshape(E, CAP, width)], axis=1
    ).astype(BF16)
    rx[cut, me] = send[lax.div(me, owners)]

    pl.semaphore_wait(barrier, (n - 1) + 1 + (nx - 1))

    def remote(src, dst, send_sem, recv_sem, device):
        return pltpu.make_async_remote_copy(
            src_ref=src, dst_ref=dst, send_sem=send_sem, recv_sem=recv_sem,
            device_id=device, device_id_type=MESH,
        )

    def source(j):
        return lax.rem(me - j + n, n)

    def copy_a(j):
        to = lax.rem(me + j, n)
        return remote(send.at[lax.div(to, owners)], rx.at[cut, me], a_send.at[j], a_recv.at[j], (to, cut))

    def copy_b(j):
        s = source(j)
        return remote(rx.at[cut, s], rx.at[cut, s], b_send.at[j], b_recv.at[j], mate)

    def copy_c(i, j):
        s = source(j)
        to = (me, lax.rem(xx + i, nx) * 2 + core)
        return remote(rx.at[cut, s], rx.at[cut, s], c_send.at[i - 1, j], c_recv.at[i - 1, j], to)

    def copy_f(i, j):
        s = source(j)
        part = lax.rem(xx - i + nx, nx) * 2 + core
        return remote(rx.at[part, s], rx.at[part, s], f_send.at[i - 1, j], f_recv.at[i - 1, j], mate)

    def loop(start, stop, step):
        def run(j, carry):
            step(j)
            return carry

        lax.fori_loop(start, stop, run, 0)

    def spread(j):
        for i in range(1, nx):
            copy_c(i, j).start()
        copy_b(j).start()

    def arrive(j):
        copy_a(j).wait_recv()
        spread(j)

    def forward(j):
        for i in range(1, nx):
            copy_c(i, j).wait_recv()
            copy_f(i, j).start()

    def both(j):
        arrive(j)
        forward(j - 2)

    def landed(j):
        copy_b(j).wait_recv()
        for i in range(1, nx):
            copy_f(i, j).wait_recv()

    loop(1, n, lambda j: copy_a(j).start())
    spread(0)
    arrive(1)
    acc_y[...] = jnp.zeros_like(acc_y)
    acc_dx[...] = jnp.zeros_like(acc_dx)
    loop(2, n, both)
    loop(n - 2, n, forward)
    loop(0, n, landed)

    rows = n * CAP
    lanes = turned_dy.shape[1]

    def turn(value, filler):
        value = value if lanes == rows else jnp.concatenate([value, filler], axis=0)
        return value.T.astype(BF16)

    for part in range(cuts):
        cols = slice(part * width, (part + 1) * width)
        got = rx[part].astype(F32)
        rows_x[:, cols] = got[:, :CAP].reshape(n * CAP, width).astype(BF16)
        turned_dy[cols, :] = turn(got[:, CAP:].reshape(rows, width), got[:, :CAP].reshape(rows, width))

    def hidden_tile(t):
        slot = lax.rem(t, depth)
        for copy in fetch(t, slot):
            copy.wait()
        gate_pre = jnp.dot(rows_x[...], wg[slot], preferred_element_type=F32)
        up_pre = jnp.dot(rows_x[...], wu[slot], preferred_element_type=F32)
        hid_grad = jnp.dot(w2[slot], turned_dy[...], preferred_element_type=F32).T[:rows]
        sigma = 1.0 / (1.0 + jnp.exp(-gate_pre))
        silu = gate_pre * sigma
        hidden = (silu * up_pre).astype(BF16)
        gate_grad = (hid_grad * up_pre * sigma * (1.0 + gate_pre * (1.0 - sigma)))
        up_grad = hid_grad * silu
        turned_gate = turn(gate_grad, up_grad)
        turned_up = turn(up_grad, gate_grad)
        for part in range(cuts):
            cols = slice(part * width, (part + 1) * width)
            acc_y[:, cols] += jnp.dot(hidden, w2[slot, :, cols], preferred_element_type=F32)
            acc_dx[cols, :] += jnp.dot(
                wg[slot, cols, :], turned_gate, preferred_element_type=F32
            ) + jnp.dot(wu[slot, cols, :], turned_up, preferred_element_type=F32)

        @pl.when(t + depth < tiles)
        def _():
            for copy in fetch(t + depth, slot):
                copy.start()

    loop(0, tiles, hidden_tile)

    def partial(part):
        cols = pl.ds(pl.multiple_of(part * width, 128), width)
        return jnp.concatenate(
            [acc_y[:, cols].reshape(n, CAP, width), acc_dx[cols, :].T[:rows].reshape(n, CAP, width)],
            axis=1,
        )

    def copy_r1(p):
        return remote(core_tx.at[p], core_rx.at[p], r1_send.at[p], r1_recv.at[p], mate)

    def copy_r2(i, d):
        to = (me, lax.rem(xx + i, nx) * 2 + core)
        return remote(
            x_tx.at[i - 1, d], x_rx.at[i - 1, d], r2_send.at[i - 1, d], r2_recv.at[i - 1, d], to
        )

    def copy_r3(j):
        to = lax.rem(me + j, n)
        return remote(back_tx.at[to], back_rx.at[me], r3_send.at[j], r3_recv.at[j], (to, cut))

    for i in list(range(1, nx)) + [0]:
        p = lax.rem(xx + i, nx)
        core_tx[p] = partial(p * 2 + 1 - core).astype(BF16)
        copy_r1(p).start()
    for i in list(range(1, nx)) + [0]:
        p = lax.rem(xx + i, nx)
        mine = partial(p * 2 + core)
        copy_r1(p).wait_recv()
        mine = mine + core_rx[p].astype(F32)
        if i == 0:
            own[...] = mine
        else:
            x_tx[i - 1] = mine.astype(BF16)
            loop(1, n + 1, lambda j, i=i: copy_r2(i, lax.rem(me + j, n)).start())

    def total(d):
        value = own[d]
        for i in range(1, nx):
            copy_r2(i, d).wait_recv()
            value = value + x_rx[i - 1, d].astype(F32)
        return value.astype(BF16)

    def give_back(j):
        d = lax.rem(me + j, n)
        back_tx[d] = total(d)
        copy_r3(j).start()

    loop(1, n, give_back)
    back_rx[me] = total(me)
    loop(1, n, lambda j: copy_r3(j).wait_recv())

    back = back_rx[...].astype(F32).reshape(E, owners, 2 * CAP, width)
    mixed = jnp.zeros(mixed_ref.shape, F32)
    grad = jnp.zeros(grad_ref.shape, F32)
    for o in range(owners):
        y = back[:, o, :CAP].reshape(E * CAP, width).astype(BF16)
        dx = back[:, o, CAP:].reshape(E * CAP, width).astype(BF16)
        mixed += gate[:, 0:1] * jnp.dot(give0[...], y, preferred_element_type=F32)
        mixed += gate[:, 1:2] * jnp.dot(give1[...], y, preferred_element_type=F32)
        grad += jnp.dot(give0[...] + give1[...], dx, preferred_element_type=F32)
    mixed_ref[...] = mixed.astype(BF16)
    grad_ref[...] = grad.astype(BF16)

    loop(1, n, lambda j: copy_a(j).wait_send())
    loop(0, n, lambda j: copy_b(j).wait_send())
    for i in range(1, nx):
        loop(0, n, lambda j, i=i: copy_c(i, j).wait_send())
        loop(0, n, lambda j, i=i: copy_f(i, j).wait_send())
        loop(0, n, lambda j, i=i: copy_r2(i, j).wait_send())
    for p in range(nx):
        copy_r1(p).wait_send()
    loop(1, n, lambda j: copy_r3(j).wait_send())


def on_device(n, cuts, tokens, out_grad, gate_values, routing, gate_weight, up_weight, down_weight):
    tables = slot_table(routing)
    count, width = tokens.shape
    _, model, hid = gate_weight.shape
    tile = 256 if hid % 256 == 0 else hid
    depth = min(4, hid // tile)
    nx, rows = cuts // 2, n * CAP
    lanes = rows if rows % 128 == 0 else 2 * rows
    chunk = (2 * CAP, width)
    dma = pltpu.SemaphoreType.DMA
    vmem = pl.BlockSpec(memory_space=pltpu.VMEM)
    hbm = pl.BlockSpec(memory_space=pl.ANY)
    out = jax.ShapeDtypeStruct((count, width), BF16)
    return pl.pallas_call(
        functools.partial(body, n, cuts, tile, depth),
        out_shape=(out, out),
        in_specs=[vmem] * 7 + [hbm] * 3,
        out_specs=(vmem, vmem),
        scratch_shapes=[
            pltpu.VMEM((depth, model, tile), BF16),
            pltpu.VMEM((depth, model, tile), BF16),
            pltpu.VMEM((depth, tile, model), BF16),
            pltpu.VMEM((E,) + chunk, BF16),
            pltpu.VMEM((cuts, n) + chunk, BF16),
            pltpu.VMEM((rows, model), BF16),
            pltpu.VMEM((model, lanes), BF16),
            pltpu.VMEM((rows, model), F32),
            pltpu.VMEM((model, lanes), F32),
            pltpu.VMEM((nx, n) + chunk, BF16),
            pltpu.VMEM((nx, n) + chunk, BF16),
            pltpu.VMEM((nx - 1, n) + chunk, BF16),
            pltpu.VMEM((nx - 1, n) + chunk, BF16),
            pltpu.VMEM((n,) + chunk, F32),
            pltpu.VMEM((n,) + chunk, BF16),
            pltpu.VMEM((n,) + chunk, BF16),
            dma((3, depth)),
            dma((n,)), dma((n,)),
            dma((n,)), dma((n,)),
            dma((nx - 1, n)), dma((nx - 1, n)),
            dma((nx - 1, n)), dma((nx - 1, n)),
            dma((nx,)), dma((nx,)),
            dma((nx - 1, n)), dma((nx - 1, n)),
            dma((n,)), dma((n,)),
        ],
        compiler_params=pltpu.CompilerParams(
            collective_id=0, has_side_effects=True, vmem_limit_bytes=62 * 1024 * 1024
        ),
        cost_estimate=pl.CostEstimate(
            flops=12 * rows * model * hid, bytes_accessed=6 * model * hid, transcendentals=rows * hid
        ),
    )(tokens, out_grad, gate_values, *tables, gate_weight, up_weight, down_weight)


def solution(mesh):
    return jax.shard_map(
        functools.partial(on_device, mesh.shape["dp"], mesh.shape["cuts"]),
        mesh=mesh,
        in_specs=(
            P("dp", "cuts"),
            P("dp", "cuts"),
            P("dp", None),
            P("dp", None),
            P("dp", None, "cuts"),
            P("dp", None, "cuts"),
            P("dp", "cuts", None),
        ),
        out_specs=(P("dp", "cuts"), P("dp", "cuts")),
        check_vma=False,
    )
```
